256 devices in a mesh: grp: 16 (over x, y_hi, core), blk: 16 (over y_lo, z).
Axes of the slice: x: 4, y: 4 (y_hi: 2, y_lo: 2; y = y_hi * 2 + y_lo), z: 8, core: 2. Of those that a mesh axis runs over, the one named last changes fastest.
Arguments:
- embeddings: bfloat16 [65536, 512], P(('grp', 'blk'))
- cluster: int32 [65536], P(('grp', 'blk')), may hold values from 0 to 47, as said below
- order: int32 [65536], P(('grp', 'blk')), may hold values from 0 to 65535, each once
Outputs:
- nearest: float32 [65536], P(('grp', 'blk'))
The draws below stay inside these ranges and needn't reach their ends.
Inputs may be any that keep to these rules, and one draw needn't show every extreme that they name: Cluster c belongs to cluster set c // 3. The 256 rows of one device hold at most 48 rows of any one cluster set, and in every draw exactly 48 rows of some set.
All inputs are finite; a program needn't handle non-finite values.
Results may differ from the reference program's by a relative error of at most 0.00057.
Values may be sent and summed in bfloat16 or wider, within the bound.
A program may use at most 64 MiB of HBM per device.

```python
import jax
import jax.numpy as jnp
from jax import lax

D = 512
ROW_DEV = 256
CL_GRP = 3
CLUSTERS = 48
ROWS = 65536
N_GRP = 16


def shared_clusters(key):
    k_heavy, k_perm, k_pick = jax.random.split(key, 3)
    heavy = jax.random.randint(k_heavy, (), 0, N_GRP)
    share = ROW_DEV // N_GRP
    place = jnp.arange(ROW_DEV)
    rest = (place - 3 * share) % (N_GRP - 1)
    other = rest + (rest >= heavy).astype(jnp.int32)
    target = jnp.where(place < 3 * share, heavy, other).astype(jnp.int32)
    devices = ROWS // ROW_DEV
    perm_keys = jax.random.split(k_perm, devices)
    shuffled = jax.vmap(lambda k: jax.random.permutation(k, target))(perm_keys)
    pick = jax.random.randint(k_pick, (ROWS,), 0, CL_GRP)
    return (shuffled.reshape(ROWS) * CL_GRP + pick).astype(jnp.int32)


def draw_cluster(key, part):
    return shared_clusters(key)


def draw_embeddings(key, part):
    labels = shared_clusters(key)
    key = jax.random.fold_in(key, 7)
    k_center, k_scale, k_noise, k_pert, k_tie, k_kept, k_cos = jax.random.split(key, 7)
    centers = jax.random.normal(k_center, (CLUSTERS, D), jnp.float32)
    noise = jax.random.normal(k_noise, (ROWS, D), jnp.float32)
    perturb = jax.random.normal(k_pert, (ROWS, D), jnp.float32)
    scale = jnp.exp(jax.random.uniform(k_scale, (ROWS, 1), jnp.float32, jnp.log(1.0), jnp.log(10.0)))
    base = 0.65 * centers[labels] + noise
    tiebreak = jax.random.permutation(k_tie, ROWS).astype(jnp.int32)
    sort_keys = labels * ROWS + tiebreak
    sorted_rows = jnp.argsort(sort_keys, stable=True).astype(jnp.int32)
    sorted_labels = labels[sorted_rows]
    counts = jnp.zeros((CLUSTERS,), jnp.int32).at[labels].add(1)
    starts = jnp.cumsum(counts) - counts
    position = jnp.arange(ROWS, dtype=jnp.int32)
    within_run = position - starts[sorted_labels]
    kept = jax.random.randint(k_kept, (ROWS,), 0, 5) > 0
    copy_sorted = (within_run % 2 == 1) & kept
    previous = sorted_rows[jnp.maximum(position - 1, 0)]
    is_copy = jnp.zeros((ROWS,), jnp.bool_).at[sorted_rows].set(copy_sorted)
    source_row = jnp.zeros((ROWS,), jnp.int32).at[sorted_rows].set(previous)
    cosine = jax.random.uniform(k_cos, (ROWS, 1), jnp.float32, 0.85, 0.99)
    spread_size = 1.2 * jnp.sqrt(1.0 / (cosine * cosine) - 1.0)
    copied = base[source_row] + spread_size * perturb
    result = jnp.where(is_copy[:, None], copied, base)
    return (scale * result).astype(jnp.bfloat16)


def setup_inputs(seed: int = 0) -> dict:
    key_of = jax.random.split(jax.random.key(seed), 4)
    embeddings = draw_embeddings(jax.random.fold_in(key_of[3], 71), 0)
    cluster = draw_cluster(jax.random.fold_in(key_of[3], 71), 0)
    order = jax.random.permutation(key_of[2], ROWS).astype(jnp.int32)
    return {"embeddings": embeddings, "cluster": cluster, "order": order}


def reference(embeddings, cluster, order):
    values = embeddings.astype(jnp.float32)
    unit = (values * lax.rsqrt(lax.optimization_barrier(jnp.sum(values * values, axis=1, keepdims=True)) + 1e-06)).astype(jnp.bfloat16)
    whole = unit.astype(jnp.float32)
    query_unit = whole.reshape(ROWS // 512, 512, D)
    query_cl = cluster.reshape(ROWS // 512, 512)
    query_ord = order.reshape(ROWS // 512, 512)

    def one_block(pieces):
        q_unit, q_cl, q_ord = pieces
        score = jnp.dot(q_unit, whole.T, precision=lax.Precision.HIGHEST)
        keep = (q_cl[:, None] == cluster[None, :]) & (order[None, :] < q_ord[:, None])
        return lax.optimization_barrier(jnp.max(jnp.where(keep, score, jnp.float32(-1.0)), axis=1))
    nearest = lax.map(one_block, (query_unit, query_cl, query_ord))
    return nearest.reshape(ROWS)
```

```python
import jax
import jax.numpy as jnp
from jax import lax
from jax.experimental import pallas as pl
from jax.experimental.pallas import tpu as pltpu
from jax.sharding import PartitionSpec as P

MESH = pl.DeviceIdType.MESH
ROWS, WIDTH, HEAD = 256, 512, 16
TALL = ROWS + HEAD
CHUNKS = ((0, 80), (80, 64), (144, 64), (208, 64))
RING = 8
SLOTS = [(0, 0, z) for z in range(8)] + [
    (1, 0, 0), (0, 3, 0), (2, 0, 0), (1, 3, 0), (3, 3, 0), (0, 2, 0), (2, 1, 0), (3, 2, 0), (2, 2, 0),
]
STEP = {"+x": (1, 0, 0), "-x": (3, 0, 0), "+y": (0, 1, 0), "-y": (0, 3, 0), "+z": (0, 0, 1), "-z": (0, 0, 7)}
TREE = {
    (0, 0, 1): ((0, 0, 0), "+z"), (0, 0, 2): ((0, 0, 1), "+z"), (0, 0, 3): ((0, 0, 2), "+z"),
    (0, 0, 7): ((0, 0, 0), "-z"), (0, 0, 6): ((0, 0, 7), "-z"), (0, 0, 5): ((0, 0, 6), "-z"),
    (0, 0, 4): (((0, 0, 3), "+z"), ((0, 0, 5), "-z")),
    (1, 0, 0): ((0, 0, 0), "+x"), (0, 3, 0): ((0, 0, 0), "-y"), (2, 0, 0): ((1, 0, 0), "+x"),
    (1, 3, 0): ((0, 3, 0), "+x"), (3, 3, 0): ((0, 3, 0), "-x"), (0, 2, 0): ((0, 3, 0), "-y"),
    (2, 1, 0): ((2, 0, 0), "+y"), (3, 2, 0): ((3, 3, 0), "-y"), (2, 2, 0): ((3, 2, 0), "-x"),
}
NS = len(SLOTS)
NC = len(CHUNKS)
WRAP = (4, 4, 8)


def plus(a, b):
    return tuple((p + q) % w for p, q, w in zip(a, b, WRAP))


def minus(a):
    return tuple((-p) % w for p, w in zip(a, WRAP))


def edges():
    out = {}
    for s in range(1, NS):
        for c in range(NC):
            t = TREE[SLOTS[s]]
            if not isinstance(t[1], str):
                t = t[c % 2]
            out[s, c] = (SLOTS.index(t[0]), t[1])
            assert plus(t[0], STEP[t[1]]) == SLOTS[s]
    return out


EDGE = edges()
KIDS = {}
for (s_, c_), (p_, u_) in EDGE.items():
    KIDS.setdefault((p_, c_), []).append((s_, u_))


def arrivals(block=4.8, hop=2.2):
    need = {}
    for s, c in EDGE:
        n, k = 0, (s, c)
        while k[0]:
            n, k = n + 1, (EDGE[k][0], c)
        need[s, c] = n
    tall = {k: 0 for k in EDGE}
    for s, c in EDGE:
        k = (s, c)
        while k[0]:
            tall[k] = max(tall[k], need[s, c] - need[k])
            k = (EDGE[k][0], c)
    at = {(0, c): 0.0 for c in range(NC)}
    free = {u: 0.0 for u in STEP}
    left = set(EDGE)
    while left:
        ready = [
            (max(at[EDGE[k][0], k[1]], free[EDGE[k][1]]), -tall[k], k[1], k[0]) for k in left if (EDGE[k][0], k[1]) in at
        ]
        t, _, c, s = min(ready)
        free[EDGE[s, c][1]] = t + block / NC
        at[s, c] = t + block / NC + hop
        left.remove((s, c))
    return at


HALF_TURN = [s for s in range(RING, NS) if plus(SLOTS[s], SLOTS[s]) == (0, 0, 0)]


def pair_tasks():
    out = [(0, a) for a in (1, 2, 3)]
    for s in range(RING, NS):
        out += [(s, a) for a in ((1, 2, 3) if s in HALF_TURN else range(RING))]
    return out


HOME = [(s, 0) for s in range(RING, NS)] + [(a, f) for a in range(1, RING) for f in (0, 1)] + [(0, 1)]


def plan():
    at = arrivals()
    seen = sorted((t, s, c) for (s, c), t in at.items() if s)
    whole = {s: max(at[s, c] for c in range(NC)) for s in range(NS)}
    ready = {t: max(whole[t[0]], whole[t[1]] + 1.5) for t in pair_tasks()}
    halves = {(s, a): max(whole[s], whole[a] + 1.5) for s in HALF_TURN for a in (0, 4)}
    halves[0, 4] = whole[4] + 1.5
    todo = sorted(ready, key=lambda t: ready[t])
    steps, now = [], 0.0
    left_h = sorted(halves, key=lambda t: halves[t])
    while todo or left_h:
        while seen and seen[0][0] <= now:
            _, s, c = seen.pop(0)
            steps.append(("chunk", s, c))
        able = [t for t in todo if ready[t] <= now][:4]
        if len(able) % 2 and len(able) > 1:
            able = able[:-1]
        if len(able) >= 2:
            steps.append(("tasks", able))
            todo = [t for t in todo if t not in able]
            now += 0.28 * len(able)
        elif left_h and halves[left_h[0]] <= now:
            steps.append(("half", left_h.pop(0)))
            now += 0.25
        elif not seen and len(able) == 1:
            steps.append(("tasks", able))
            todo = [t for t in todo if t not in able]
            now += 0.3
        elif seen:
            now = seen[0][0]
        else:
            now += 0.25
    return steps


def pick(table, i):
    value = jnp.int32(table[-1])
    for k in range(len(table) - 2, -1, -1):
        if table[k] != table[-1]:
            value = jnp.where(i == k, jnp.int32(table[k]), value)
    return value


def kernel(x_ref, cl_ref, ord_ref, out_ref, buf, row_cl, row_ord, col_cl, col_ord, row_best, col_best, score,
           send_back, got_back, link_out, link_in, pair_out, pair_in, home_out, home_in):
    g, b = lax.axis_index("grp"), lax.axis_index("blk")
    core = g % 2
    here = (g // 4, ((g // 2) % 2) * 2 + b // 8, b % 8)

    def device(d, flip=0):
        x, y, z = ((h + k) % w for h, k, w in zip(here, d, WRAP))
        return ((x * 2 + y // 2) * 2 + (1 - core if flip else core), (y % 2) * 8 + z)

    goes = {(minus(STEP[u]), 0) for u in STEP} | {((0, 0, 0), 1)} | {(SLOTS[s], f) for s, f in HOME}
    comes = {(minus(d), f) for d, f in goes}
    barrier = pltpu.get_barrier_semaphore()
    for d, f in sorted(comes):
        pl.semaphore_signal(barrier, inc=1, device_id=device(d, f), device_id_type=MESH)

    values = x_ref[...].astype(jnp.float32)
    scale = lax.rsqrt(jnp.sum(values * values, axis=1, keepdims=True) + 1e-06)
    buf[0, 0, pl.ds(HEAD, ROWS), :] = (values * scale).astype(jnp.bfloat16)
    line = lax.broadcasted_iota(jnp.int32, (HEAD, ROWS), 0)
    rank = ord_ref[...]
    head = jnp.where(line == 0, cl_ref[...], jnp.where(line == 1, rank // 256, jnp.where(line == 2, rank % 256, 0)))
    head = head.astype(jnp.float32).astype(jnp.bfloat16)
    buf[0, 0, pl.ds(0, HEAD), pl.ds(0, ROWS)] = head
    buf[0, 0, pl.ds(0, HEAD), pl.ds(ROWS, WIDTH - ROWS)] = jnp.zeros((HEAD, WIDTH - ROWS), jnp.bfloat16)

    pl.semaphore_wait(barrier, len(goes))

    def hop(s, c):
        lo, n = CHUNKS[c]
        p, u = EDGE[s, c]
        return pltpu.make_async_remote_copy(
            src_ref=buf.at[0, p, pl.ds(lo, n)], dst_ref=buf.at[0, s, pl.ds(lo, n)],
            send_sem=link_out.at[s, c], recv_sem=link_in.at[s, c],
            device_id=device(minus(STEP[u])), device_id_type=MESH,
        )

    def across(a):
        return pltpu.make_async_remote_copy(
            src_ref=buf.at[0, a], dst_ref=buf.at[1, a], send_sem=pair_out.at[a], recv_sem=pair_in.at[a],
            device_id=device((0, 0, 0), 1), device_id_type=MESH,
        )

    for c in range(NC):
        for s, _ in KIDS[0, c]:
            hop(s, c).start()
    across(0).start()

    def row_slot(s):
        return 0 if s == 0 else s - RING + 1

    rows16 = lax.broadcasted_iota(jnp.int32, (HEAD, 256), 0)
    lane16 = lax.broadcasted_iota(jnp.int32, (HEAD, 256), 1)
    spread = jnp.where(
        lane16 < 128, jnp.where(rows16 == 0, 1.0, 0.0), jnp.where(rows16 == 1, 256.0, jnp.where(rows16 == 2, 1.0, 0.0))
    ).astype(jnp.bfloat16)

    def row_side(s):
        wide = lax.dot_general(
            buf[0, s, pl.ds(0, HEAD), pl.ds(0, ROWS)], spread, (((0,), (0,)), ((), ())), preferred_element_type=jnp.float32
        )
        k = row_slot(s)
        row_cl[k] = wide[:, :128]
        row_ord[k] = wide[:, 128:]

    def col_side(a, half):
        top = buf[half, a, pl.ds(0, HEAD), pl.ds(0, ROWS)].astype(jnp.float32)
        col_cl[a, half] = jnp.broadcast_to(top[0:1], (8, ROWS))
        col_ord[a, half] = jnp.broadcast_to(top[1:2] * 256.0 + top[2:3], (8, ROWS))

    row_best[...] = jnp.full(row_best.shape, -1.0, jnp.float32)
    col_best[...] = jnp.full(col_best.shape, -1.0, jnp.float32)

    def dot(s, a):
        rows = buf[0, s, pl.ds(HEAD, ROWS), :]
        columns = jnp.concatenate([buf[h, a, pl.ds(HEAD, ROWS), :] for h in (0, 1)], axis=0)
        return lax.dot_general(rows, columns, (((1,), (1,)), ((), ())), preferred_element_type=jnp.float32)

    def fold(ref, k, a, halves=(0, 1), both=True):
        tiles = [(h, t) for h in halves for t in (0, 128)]
        cl = [col_cl[a, h, :, pl.ds(t, 128)] for h, t in tiles]
        rk = [col_ord[a, h, :, pl.ds(t, 128)] for h, t in tiles]
        top = [col_best[a, h, :, pl.ds(t, 128)] for h, t in tiles] if both else None
        for i in range(ROWS // 8):
            at = pl.ds(8 * i, 8)
            mine, rank, best = row_cl[k, at, :], row_ord[k, at, :], row_best[k, at, :]
            for n in range(len(tiles)):
                s = ref[at, pl.ds(128 * n, 128)]
                same = jnp.where(mine == cl[n], s, -1.0)
                later = rk[n] < rank
                best = jnp.maximum(best, jnp.where(later, same, -1.0))
                if both:
                    top[n] = jnp.maximum(top[n], jnp.where(later, -1.0, same))
            row_best[k, at, :] = best
        if both:
            for n, (h, t) in enumerate(tiles):
                col_best[a, h, :, pl.ds(t, 128)] = top[n]

    row_side(0)
    col_side(0, 0)
    met = {0}

    def meet(a):
        if ("pair", a) not in met:
            met.add(("pair", a))
            across(a).wait_recv()
            col_side(a, 1)

    def flip(s):
        d = SLOTS[s]
        return here[0] // 2 if d[0] == 2 else (here[1] // 2 if d[1] == 2 else here[2] // 4)

    meet(0)
    score[0] = dot(0, 0)
    fold(score.at[0], 0, 0, both=False)

    parts = {s: 0 for s in range(NS)}
    for step in plan():
        if step[0] == "chunk":
            _, s, c = step
            hop(s, c).wait_recv()
            for kid, _ in KIDS.get((s, c), ()):
                hop(kid, c).start()
            parts[s] += 1
            if parts[s] == NC:
                if s < RING:
                    across(s).start()
                    col_side(s, 0)
                else:
                    row_side(s)
        elif step[0] == "half":
            s, a = step[1]
            meet(a)
            f = flip(s if s else 4)
            score[0, :, pl.ds(0, ROWS)] = lax.dot_general(
                buf[0, s, pl.ds(HEAD, ROWS), :], buf[f, a, pl.ds(HEAD, ROWS), :], (((1,), (1,)), ((), ())),
                preferred_element_type=jnp.float32,
            )
            fold(score.at[0], row_slot(s), a, halves=(f,))
        else:
            tasks = step[1]
            for _, a in tasks:
                meet(a)
            if len(tasks) == 1:
                score[0] = dot(*tasks[0])
                fold(score.at[0], row_slot(tasks[0][0]), tasks[0][1])
                continue
            n = len(tasks)
            row_at, col_at = [t[0] for t in tasks], [t[1] for t in tasks]
            score[0] = dot(*tasks[0])

            def pair(j, carry, row_at=row_at, col_at=col_at, n=n):
                def task(i):
                    return pick(row_at, i), pick(col_at, i)

                def slot_of(s):
                    return jnp.where(s == 0, 0, s - RING + 1)

                first, second = task(2 * j), task(2 * j + 1)
                score[1] = dot(*second)
                fold(score.at[0], slot_of(first[0]), first[1])
                if n > 2:
                    score[0] = dot(*task(2 * j + 2))
                fold(score.at[1], slot_of(second[0]), second[1])
                return carry

            lax.fori_loop(0, n // 2, pair, 0)

    def row_result(k):
        m = row_best[k]
        return jnp.concatenate(
            [jnp.max(m[128 * h : 128 * h + 128].T, axis=0, keepdims=True) for h in (0, 1)], axis=1
        )

    def col_result(a, h):
        return jnp.max(col_best[a, h], axis=0, keepdims=True)

    def home(n):
        s, f = HOME[n]
        return pltpu.make_async_remote_copy(
            src_ref=send_back.at[n], dst_ref=got_back.at[n], send_sem=home_out.at[n], recv_sem=home_in.at[n],
            device_id=device(SLOTS[s], f), device_id_type=MESH,
        )

    for n, (s, f) in enumerate(HOME):
        send_back[n] = row_result(row_slot(s)) if s >= RING else col_result(s, f)
        home(n).start()
    best = jnp.maximum(row_result(0), col_result(0, 0))
    for n in range(len(HOME)):
        home(n).wait_recv()
        best = jnp.maximum(best, got_back[n])
    out_ref[...] = best
    for s, c in EDGE:
        hop(s, c).wait_send()
    for a in range(RING):
        across(a).wait_send()
    for n in range(len(HOME)):
        home(n).wait_send()


def body(embeddings, cluster, order):
    f32, nr, nh = jnp.float32, NS - RING + 1, len(HOME)
    dma = pltpu.SemaphoreType.DMA
    out = pl.pallas_call(
        kernel,
        out_shape=jax.ShapeDtypeStruct((1, ROWS), f32),
        in_specs=[pl.BlockSpec(memory_space=pltpu.VMEM)] * 3,
        out_specs=pl.BlockSpec(memory_space=pltpu.VMEM),
        scratch_shapes=[
            pltpu.VMEM((2, NS, TALL, WIDTH), jnp.bfloat16),
            pltpu.VMEM((nr, ROWS, 128), f32), pltpu.VMEM((nr, ROWS, 128), f32),
            pltpu.VMEM((RING, 2, 8, ROWS), f32), pltpu.VMEM((RING, 2, 8, ROWS), f32),
            pltpu.VMEM((nr, ROWS, 128), f32), pltpu.VMEM((RING, 2, 8, ROWS), f32),
            pltpu.VMEM((2, ROWS, 2 * ROWS), f32),
            pltpu.VMEM((nh, 1, ROWS), f32), pltpu.VMEM((nh, 1, ROWS), f32),
            dma((NS, NC)), dma((NS, NC)), dma((RING,)), dma((RING,)), dma((nh,)), dma((nh,)),
        ],
        compiler_params=pltpu.CompilerParams(collective_id=0, has_side_effects=True, vmem_limit_bytes=40 * 2**20),
        cost_estimate=pl.CostEstimate(flops=10**10, bytes_accessed=2**20, transcendentals=0),
        name="nearest",
    )(embeddings, cluster.reshape(1, ROWS), order.reshape(1, ROWS))
    return out.reshape(ROWS)


def solution(mesh):
    return jax.shard_map(
        body,
        mesh=mesh,
        in_specs=(P(("grp", "blk"), None), P(("grp", "blk")), P(("grp", "blk"))),
        out_specs=P(("grp", "blk")),
        check_vma=False,
    )
```

```python
import jax
import jax.numpy as jnp
from jax import lax
from jax.experimental import pallas as pl
from jax.experimental.pallas import tpu as pltpu
from jax.sharding import PartitionSpec as P

MESH = pl.DeviceIdType.MESH
ROWS, WIDTH = 256, 512
HEAD = (16, 128)
CHUNKS = ((0, 64), (64, 64), (128, 64), (192, 64))
RING = 8
SLOTS = [(0, 0, z) for z in range(8)] + [
    (1, 0, 0), (0, 1, 0), (1, 1, 0), (1, 3, 0), (2, 0, 0), (0, 2, 0), (2, 1, 0), (3, 2, 0), (2, 2, 0),
]
NR = len(SLOTS) - RING + 1
SLOTS += [(3, 0, 0), (0, 3, 0)]
STEP = {"+x": (1, 0, 0), "-x": (3, 0, 0), "+y": (0, 1, 0), "-y": (0, 3, 0), "+z": (0, 0, 1), "-z": (0, 0, 7)}
FROM = {
    (0, 0, 1): ("+z", "+z"), (0, 0, 2): ("+z", "+z"), (0, 0, 3): ("+z", "+z"),
    (0, 0, 7): ("-z", "-z"), (0, 0, 6): ("-z", "-z"), (0, 0, 5): ("-z", "-z"), (0, 0, 4): ("+z", "-z"),
    (1, 0, 0): ("+x", "+x"), (3, 0, 0): ("-x", "-x"), (0, 1, 0): ("+y", "+y"), (0, 3, 0): ("-y", "-y"),
    (2, 0, 0): ("+x", "-x"), (0, 2, 0): ("+y", "-y"), (1, 1, 0): ("+x", "+y"), (1, 3, 0): ("-y", "-y"),
    (2, 1, 0): ("+x", "+y"), (3, 2, 0): ("-x", "-x"), (2, 2, 0): ("-x", "+y"),
}
NS = len(SLOTS)
NC = len(CHUNKS)
WRAP = (4, 4, 8)


def plus(a, b):
    return tuple((p + q) % w for p, q, w in zip(a, b, WRAP))


def minus(a):
    return tuple((-p) % w for p, w in zip(a, WRAP))


EDGE = {}
for s_ in range(1, NS):
    for c_ in range(NC):
        u_ = FROM[SLOTS[s_]][c_ % 2]
        EDGE[s_, c_] = (SLOTS.index(plus(SLOTS[s_], minus(STEP[u_]))), u_)
KIDS = {}
for (s_, c_), (p_, u_) in EDGE.items():
    KIDS.setdefault((p_, c_), []).append(s_)


def depth(s, c):
    return 0 if s == 0 else 1 + depth(EDGE[s, c][0], c)


def height(s, c):
    return max([0] + [1 + height(k, c) for k in KIDS.get((s, c), ())])


def arrivals(block=5.3, hop=2.0):
    at = {(0, c): 0.0 for c in range(NC)}
    free = {u: 0.0 for u in STEP}
    left = set(EDGE)
    while left:
        ready = [
            (max(at[EDGE[k][0], k[1]], free[EDGE[k][1]]), at[EDGE[k][0], k[1]], k[1], -height(*k), k[0])
            for k in left if (EDGE[k][0], k[1]) in at
        ]
        t, _, c, _, s = min(ready)
        free[EDGE[s, c][1]] = t + block / NC
        at[s, c] = t + block / NC + hop
        left.remove((s, c))
    return at


HALF_TURN = [s for s in range(RING, RING + NR - 1) if plus(SLOTS[s], SLOTS[s]) == (0, 0, 0)]
HOME = [(s, 0) for s in range(RING, RING + NR - 1)] + [(a, f) for a in range(1, RING) for f in (0, 1)] + [(0, 1)]
ITEM = 0.47


def slot_of(k):
    return 0 if k == 0 else k + RING - 1


def items(whole):
    out = []
    for a in range(RING):
        ks = [k for k in range(NR) if not (k == 0 and a in (0, 5, 6, 7)) and not (slot_of(k) in HALF_TURN and a > 4)]
        ks.sort(key=lambda k: whole[slot_of(k)])
        if len(ks) % 2:
            ks.append(ks[-1])
        for i in range(0, len(ks), 2):
            at = max(whole[slot_of(ks[i])], whole[slot_of(ks[i + 1])], whole[a] + 1.7)
            out.append((at, ks[i], ks[i + 1], a))
    return sorted(out)


def plan():
    at = arrivals()
    seen = sorted((t, c, s) for (s, c), t in at.items() if s)
    whole = {s: max(at[s, c] for c in range(NC)) for s in range(NS)}
    todo = items(whole)
    steps, now, pending, home_left = [], 0.7, None, list(range(len(HOME)))

    def homes():
        left = [i[1:] for i in todo] + ([pending] if pending else [])
        for n in list(home_left):
            s = HOME[n][0]
            if any(s == i[2] or s in (slot_of(i[0]), slot_of(i[1])) for i in left):
                continue
            steps.append(("home", n))
            home_left.remove(n)

    while todo:
        while seen and seen[0][0] <= now:
            _, c, s = seen.pop(0)
            steps.append(("chunk", s, c))
        able = [i for i in todo if i[0] <= now]
        if able and pending is None:
            steps.append(("first", able[0][1:]))
            pending = able[0][1:]
            todo.remove(able[0])
            now += ITEM / 2
            continue
        if seen:
            able = able[:2]
        able = able[: len(able) // 2 * 2]
        if len(todo) == 1 and not able and todo[0][0] <= now:
            able = todo[:1]
        if able:
            steps.append(("items", [pending] + [i[1:] for i in able]))
            pending = able[-1][1:]
            todo = [i for i in todo if i not in able]
            now += ITEM * len(able)
            if not len(able) % 2:
                homes()
        elif pending is not None and (not seen or seen[0][0] > now + 0.5):
            steps.append(("last", pending))
            pending = None
            now += ITEM / 2
        elif seen:
            now = max(now, seen[0][0])
        else:
            now += 0.1
    assert not seen
    if pending is not None:
        steps.append(("last", pending))
        pending = None
    homes()
    assert not home_left
    return steps


def pick(table, i):
    value = jnp.int32(table[-1])
    for k in range(len(table) - 2, -1, -1):
        if table[k] != table[-1]:
            value = jnp.where(i == k, jnp.int32(table[k]), value)
    return value


def kernel(x_hbm, cl_hbm, ord_hbm, out_ref, x_ref, cl_ref, ord_ref, buf, head, row_cl, row_ord, col_cl, col_ord, row_best,
           col_best, score_a, score_b, send_back, got_back, own_in, link_out, link_in, head_out, head_in, pair_out, pair_in,
           pair_head_out, pair_head_in, home_out, home_in):
    g, b = lax.axis_index("grp"), lax.axis_index("blk")
    core = g % 2
    here = (g // 4, ((g // 2) % 2) * 2 + b // 8, b % 8)
    f32, bf16 = jnp.float32, jnp.bfloat16

    loads = [
        pltpu.make_async_copy(a, v, own_in.at[n])
        for n, (a, v) in enumerate(((x_hbm, x_ref), (cl_hbm, cl_ref), (ord_hbm, ord_ref)))
    ]
    for load in loads:
        load.start()

    def device(d, flip=0):
        x, y, z = ((h + k) % w for h, k, w in zip(here, d, WRAP))
        return ((x * 2 + y // 2) * 2 + (1 - core if flip else core), (y % 2) * 8 + z)

    goes = {(minus(STEP[u]), 0) for u in STEP} | {((0, 0, 0), 1)} | {(SLOTS[s], f) for s, f in HOME}
    comes = {(minus(d), f) for d, f in goes}
    barrier = pltpu.get_barrier_semaphore()
    for d, f in sorted(comes):
        pl.semaphore_signal(barrier, inc=1, device_id=device(d, f), device_id_type=MESH)

    row_best[...] = jnp.full(row_best.shape, -1.0, f32)
    col_best[...] = jnp.full(col_best.shape, -1.0, f32)
    for load in loads:
        load.wait()
    values = x_ref[...].astype(f32)
    scale = lax.rsqrt(jnp.sum(values * values, axis=1, keepdims=True) + 1e-06)
    buf[0, 0] = (values * scale).astype(bf16)
    line = lax.broadcasted_iota(jnp.int32, HEAD, 0)
    facts = jnp.zeros(HEAD, jnp.int32)
    for h in (0, 1):
        cl, rank = cl_ref[:, pl.ds(128 * h, 128)], ord_ref[:, pl.ds(128 * h, 128)]
        for n, row in ((0, cl), (2, rank // 256), (4, rank % 256)):
            facts = jnp.where(line == n + h, row, facts)
    head[0, 0] = facts.astype(f32).astype(bf16)

    pl.semaphore_wait(barrier, len(goes))

    def hop(s, c):
        lo, n = CHUNKS[c]
        p, u = EDGE[s, c]
        return pltpu.make_async_remote_copy(
            src_ref=buf.at[0, p, pl.ds(lo, n)], dst_ref=buf.at[0, s, pl.ds(lo, n)],
            send_sem=link_out.at[s, c], recv_sem=link_in.at[s, c],
            device_id=device(minus(STEP[u])), device_id_type=MESH,
        )

    def head_hop(s):
        p, u = EDGE[s, 0]
        return pltpu.make_async_remote_copy(
            src_ref=head.at[0, p], dst_ref=head.at[0, s], send_sem=head_out.at[s], recv_sem=head_in.at[s],
            device_id=device(minus(STEP[u])), device_id_type=MESH,
        )

    def across(a):
        return [
            pltpu.make_async_remote_copy(
                src_ref=ref.at[0, a], dst_ref=ref.at[1, a], send_sem=out.at[a], recv_sem=into.at[a],
                device_id=device((0, 0, 0), 1), device_id_type=MESH,
            )
            for ref, out, into in ((buf, pair_out, pair_in), (head, pair_head_out, pair_head_in))
        ]

    def send_on(s, c):
        for kid in sorted(KIDS.get((s, c), ()), key=lambda k: -height(k, c)):
            if c == 0:
                head_hop(kid).start()
            hop(kid, c).start()

    for c in range(NC):
        send_on(0, c)
    for copy in across(0):
        copy.start()

    lines = lax.broadcasted_iota(jnp.int32, (HEAD[0], 256), 0)
    lanes = lax.broadcasted_iota(jnp.int32, (HEAD[0], 256), 1)

    def spread(h):
        low = jnp.where(lines == h, 1.0, 0.0)
        high = jnp.where(lines == 2 + h, 256.0, jnp.where(lines == 4 + h, 1.0, 0.0))
        return jnp.where(lanes < 128, low, high).astype(bf16)

    def row_side(s):
        k = 0 if s == 0 else s - RING + 1
        for h in (0, 1):
            wide = lax.dot_general(head[0, s], spread(h), (((0,), (0,)), ((), ())), preferred_element_type=f32)
            row_cl[k, pl.ds(128 * h, 128), :] = wide[:, :128]
            row_ord[k, pl.ds(128 * h, 128), :] = wide[:, 128:]

    def col_side(a, half):
        top = head[half, a].astype(f32)
        for h in (0, 1):
            at = pl.ds(128 * h, 128)
            col_cl[a, half, :, at] = jnp.broadcast_to(top[h : h + 1], (8, 128))
            col_ord[a, half, :, at] = jnp.broadcast_to(top[2 + h : 3 + h] * 256.0 + top[4 + h : 5 + h], (8, 128))

    def slot(k):
        return slot_of(k) if isinstance(k, int) else jnp.where(k == 0, 0, k + RING - 1)

    def dot(item):
        *ks, a = item
        rows = jnp.concatenate([buf[0, slot(k)] for k in ks], axis=0)
        columns = jnp.concatenate([buf[0, a], buf[1, a]], axis=0)
        return lax.dot_general(rows, columns, (((1,), (1,)), ((), ())), preferred_element_type=f32)

    tiles = [(h, t) for h in (0, 1) for t in (0, 128)]

    def fold(ref, item, both=True):
        *ks, a = item
        cl = [col_cl[a, h, :, pl.ds(t, 128)] for h, t in tiles]
        rk = [col_ord[a, h, :, pl.ds(t, 128)] for h, t in tiles]
        top = [col_best[a, h, :, pl.ds(t, 128)] for h, t in tiles] if both else None
        for m, k in enumerate(ks):
            for i in range(ROWS // 8):
                at = pl.ds(8 * i, 8)
                mine, rank, best = row_cl[k, at, :], row_ord[k, at, :], row_best[k, at, :]
                for n in range(len(tiles)):
                    s = ref[pl.ds(ROWS * m + 8 * i, 8), pl.ds(128 * n, 128)]
                    same = jnp.where(mine == cl[n], s, -1.0)
                    later = rk[n] < rank
                    best = jnp.maximum(best, jnp.where(later, same, -1.0))
                    if both:
                        top[n] = jnp.maximum(top[n], jnp.where(later, -1.0, same))
                row_best[k, at, :] = best
        if both:
            for n, (h, t) in enumerate(tiles):
                col_best[a, h, :, pl.ds(t, 128)] = top[n]

    met = set()

    def meet(a):
        if a not in met:
            met.add(a)
            for copy in across(a):
                copy.wait_recv()
            col_side(a, 1)

    def row_result(k):
        m = row_best[k]
        return jnp.concatenate(
            [jnp.max(m[128 * h : 128 * h + 128].T, axis=0, keepdims=True) for h in (0, 1)], axis=1
        )

    def col_result(a, h):
        return jnp.max(col_best[a, h], axis=0, keepdims=True)

    def home(n):
        s, f = HOME[n]
        return pltpu.make_async_remote_copy(
            src_ref=send_back.at[n], dst_ref=got_back.at[n], send_sem=home_out.at[n], recv_sem=home_in.at[n],
            device_id=device(SLOTS[s], f), device_id_type=MESH,
        )

    row_side(0)
    col_side(0, 0)
    meet(0)
    score_a[pl.ds(0, ROWS), :] = dot((0, 0))
    fold(score_a, (0, 0), both=False)

    parts = {s: 0 for s in range(NS)}
    for step in plan():
        if step[0] == "chunk":
            _, s, c = step
            hop(s, c).wait_recv()
            if c == 0:
                head_hop(s).wait_recv()
            send_on(s, c)
            parts[s] += 1
            if parts[s] == NC:
                if s < RING:
                    for copy in across(s):
                        copy.start()
                    col_side(s, 0)
                elif s < RING + NR - 1:
                    row_side(s)
        elif step[0] == "home":
            n = step[1]
            s, f = HOME[n]
            send_back[n] = row_result(s - RING + 1) if s >= RING else col_result(s, f)
            home(n).start()
        elif step[0] == "first":
            meet(step[1][2])
            score_a[...] = dot(step[1])
        elif step[0] == "last":
            fold(score_a, step[1])
        else:
            table = step[1]
            for i in table[1:]:
                meet(i[2])
            n = len(table) - 1
            if n == 1:
                score_b[...] = dot(table[1])
                fold(score_a, table[0])
                score_a[...] = score_b[...]
                continue

            def pair(j, item):
                score_b[...] = dot(item(2 * j + 1))
                fold(score_a, item(2 * j))
                score_a[...] = dot(item(2 * j + 2))
                fold(score_b, item(2 * j + 1))

            if n == 2:
                pair(0, lambda i, table=table: table[i])
            else:
                def turn(j, carry, table=table, pair=pair):
                    pair(j, lambda i: tuple(pick([t[m] for t in table], i) for m in range(3)))
                    return carry

                lax.fori_loop(0, n // 2, turn, 0)

    best = jnp.maximum(row_result(0), col_result(0, 0))
    for n in range(len(HOME)):
        home(n).wait_recv()
        best = jnp.maximum(best, got_back[n])
    out_ref[...] = best
    for s, c in EDGE:
        hop(s, c).wait_send()
        if c == 0:
            head_hop(s).wait_send()
    for a in range(RING):
        for copy in across(a):
            copy.wait_send()
    for n in range(len(HOME)):
        home(n).wait_send()


def body(embeddings, cluster, order):
    f32, bf16, i32, nh = jnp.float32, jnp.bfloat16, jnp.int32, len(HOME)
    dma = pltpu.SemaphoreType.DMA
    out = pl.pallas_call(
        kernel,
        out_shape=jax.ShapeDtypeStruct((1, ROWS), f32),
        in_specs=[pl.BlockSpec(memory_space=pl.ANY)] * 3,
        out_specs=pl.BlockSpec(memory_space=pltpu.VMEM),
        scratch_shapes=[
            pltpu.VMEM((ROWS, WIDTH), bf16), pltpu.VMEM((1, ROWS), i32), pltpu.VMEM((1, ROWS), i32),
            pltpu.VMEM((2, NS, ROWS, WIDTH), bf16), pltpu.VMEM((2, NS, *HEAD), bf16),
            pltpu.VMEM((NR, ROWS, 128), f32), pltpu.VMEM((NR, ROWS, 128), f32),
            pltpu.VMEM((RING, 2, 8, ROWS), f32), pltpu.VMEM((RING, 2, 8, ROWS), f32),
            pltpu.VMEM((NR, ROWS, 128), f32), pltpu.VMEM((RING, 2, 8, ROWS), f32),
            pltpu.VMEM((2 * ROWS, 2 * ROWS), f32), pltpu.VMEM((2 * ROWS, 2 * ROWS), f32),
            pltpu.VMEM((nh, 1, ROWS), f32), pltpu.VMEM((nh, 1, ROWS), f32), dma((3,)),
            dma((NS, NC)), dma((NS, NC)), dma((NS,)), dma((NS,)), dma((RING,)), dma((RING,)), dma((RING,)), dma((RING,)),
            dma((nh,)), dma((nh,)),
        ],
        compiler_params=pltpu.CompilerParams(collective_id=0, has_side_effects=True, vmem_limit_bytes=40 * 2**20),
        cost_estimate=pl.CostEstimate(flops=10**10, bytes_accessed=2**20, transcendentals=0),
        name="nearest",
    )(embeddings, cluster.reshape(1, ROWS), order.reshape(1, ROWS))
    return out.reshape(ROWS)


def solution(mesh):
    return jax.shard_map(
        body,
        mesh=mesh,
        in_specs=(P(("grp", "blk"), None), P(("grp", "blk")), P(("grp", "blk"))),
        out_specs=P(("grp", "blk")),
        check_vma=False,
    )
```

```python
import jax
import jax.numpy as jnp
from jax import lax
from jax.experimental import pallas as pl
from jax.experimental.pallas import tpu as pltpu
from jax.sharding import PartitionSpec as P

MESH = pl.DeviceIdType.MESH
ROWS, WIDTH = 256, 512
HEAD = (16, 128)
CHUNKS = ((0, 64), (64, 64), (128, 64), (192, 64))
RING = 8
SLOTS = [(0, 0, z) for z in range(8)] + [
    (1, 0, 0), (0, 1, 0), (1, 1, 0), (1, 3, 0), (2, 0, 0), (0, 2, 0), (2, 1, 0), (3, 2, 0), (2, 2, 0),
]
NR = len(SLOTS) - RING + 1
SLOTS += [(3, 0, 0), (0, 3, 0)]
STEP = {"+x": (1, 0, 0), "-x": (3, 0, 0), "+y": (0, 1, 0), "-y": (0, 3, 0), "+z": (0, 0, 1), "-z": (0, 0, 7)}
FROM = {
    (0, 0, 1): ("+z", "+z"), (0, 0, 2): ("+z", "+z"), (0, 0, 3): ("+z", "+z"),
    (0, 0, 7): ("-z", "-z"), (0, 0, 6): ("-z", "-z"), (0, 0, 5): ("-z", "-z"), (0, 0, 4): ("+z", "-z"),
    (1, 0, 0): ("+x", "+x"), (3, 0, 0): ("-x", "-x"), (0, 1, 0): ("+y", "+y"), (0, 3, 0): ("-y", "-y"),
    (2, 0, 0): ("+x", "-x"), (0, 2, 0): ("+y", "-y"), (1, 1, 0): ("+x", "+y"), (1, 3, 0): ("-y", "-y"),
    (2, 1, 0): ("+x", "+y"), (3, 2, 0): ("-x", "-x"), (2, 2, 0): ("-x", "+y"),
}
NS = len(SLOTS)
NC = len(CHUNKS)
WRAP = (4, 4, 8)


def plus(a, b):
    return tuple((p + q) % w for p, q, w in zip(a, b, WRAP))


def minus(a):
    return tuple((-p) % w for p, w in zip(a, WRAP))


EDGE = {}
for s_ in range(1, NS):
    for c_ in range(NC):
        u_ = FROM[SLOTS[s_]][c_ % 2]
        EDGE[s_, c_] = (SLOTS.index(plus(SLOTS[s_], minus(STEP[u_]))), u_)
KIDS = {}
for (s_, c_), (p_, u_) in EDGE.items():
    KIDS.setdefault((p_, c_), []).append(s_)


def depth(s, c):
    return 0 if s == 0 else 1 + depth(EDGE[s, c][0], c)


def height(s, c):
    return max([0] + [1 + height(k, c) for k in KIDS.get((s, c), ())])


def arrivals(block=5.3, hop=2.0):
    at = {(0, c): 0.0 for c in range(NC)}
    free = {u: 0.0 for u in STEP}
    left = set(EDGE)
    while left:
        ready = [
            (max(at[EDGE[k][0], k[1]], free[EDGE[k][1]]), at[EDGE[k][0], k[1]], k[1], -height(*k), k[0])
            for k in left if (EDGE[k][0], k[1]) in at
        ]
        t, _, c, _, s = min(ready)
        free[EDGE[s, c][1]] = t + block / NC
        at[s, c] = t + block / NC + hop
        left.remove((s, c))
    return at


HALF_TURN = [s for s in range(RING, RING + NR - 1) if plus(SLOTS[s], SLOTS[s]) == (0, 0, 0)]
HOME = [(s, 0) for s in range(RING, RING + NR - 1)] + [(a, f) for a in range(1, RING) for f in (0, 1)] + [(0, 1)]
ITEM = 0.45
PAIR = 1.5


def slot_of(k):
    return 0 if k == 0 else k + RING - 1


def far(s):
    return sum(min(p, w - p) for p, w in zip(SLOTS[s], WRAP))


def reach(item):
    return max(far(slot_of(item[1])), far(slot_of(item[2])), far(item[3]))


def items(whole):
    out = []
    for a in range(RING):
        ks = [k for k in range(NR) if not (k == 0 and a in (0, 5, 6, 7)) and not (slot_of(k) in HALF_TURN and a > 4)]
        ks.sort(key=lambda k: (whole[slot_of(k)], k))
        if len(ks) % 2:
            ks.append(ks[-1])
        for i in range(0, len(ks), 2):
            at = max(whole[slot_of(ks[i])], whole[slot_of(ks[i + 1])], whole[a] + PAIR)
            out.append((at, ks[i], ks[i + 1], a))
    return sorted(out)


def plan():
    at = arrivals()
    seen = sorted((t, c, s) for (s, c), t in at.items() if s)
    whole = {s: max(at[s, c] for c in range(NC)) for s in range(NS)}
    todo = items(whole)
    steps, now, pending, home_left = [], 0.7, None, list(range(len(HOME)))

    def homes():
        left = [i[1:] for i in todo] + ([pending] if pending else [])
        for n in list(home_left):
            s = HOME[n][0]
            if any(s == i[2] or s in (slot_of(i[0]), slot_of(i[1])) for i in left):
                continue
            steps.append(("home", n))
            home_left.remove(n)

    while todo:
        while seen and seen[0][0] <= now:
            _, c, s = seen.pop(0)
            steps.append(("chunk", s, c))
        able = sorted((i for i in todo if i[0] <= now), key=lambda i: (-reach(i), i))
        if able and pending is None:
            steps.append(("first", able[0][1:]))
            pending = able[0][1:]
            todo.remove(able[0])
            now += ITEM / 2
            continue
        able = able[:2]
        if len(able) == 1 and len(todo) > 1:
            able = []
        if able:
            steps.append(("items", [pending] + [i[1:] for i in able]))
            pending = able[-1][1:]
            todo = [i for i in todo if i not in able]
            now += ITEM * len(able)
            if not len(able) % 2:
                homes()
        elif pending is not None and (not seen or seen[0][0] > now + 0.5):
            steps.append(("last", pending))
            pending = None
            now += ITEM / 2
        elif seen:
            now = max(now, seen[0][0])
        else:
            now += 0.1
    assert not seen
    if pending is not None:
        steps.append(("last", pending))
        pending = None
    homes()
    assert not home_left
    return steps


def pick(table, i):
    value = jnp.int32(table[-1])
    for k in range(len(table) - 2, -1, -1):
        if table[k] != table[-1]:
            value = jnp.where(i == k, jnp.int32(table[k]), value)
    return value


def kernel(x_hbm, cl_hbm, ord_hbm, out_ref, x_ref, cl_ref, ord_ref, buf, head, row_cl, row_ord, col_cl, col_ord, row_best,
           col_best, score_a, score_b, send_back, got_back, own_in, link_out, link_in, head_out, head_in, pair_out, pair_in,
           pair_head_out, pair_head_in, home_out, home_in):
    g, b = lax.axis_index("grp"), lax.axis_index("blk")
    core = g % 2
    here = (g // 4, ((g // 2) % 2) * 2 + b // 8, b % 8)
    f32, bf16 = jnp.float32, jnp.bfloat16

    loads = [
        pltpu.make_async_copy(a, v, own_in.at[n])
        for n, (a, v) in enumerate(((x_hbm, x_ref), (cl_hbm, cl_ref), (ord_hbm, ord_ref)))
    ]
    for load in loads:
        load.start()

    def device(d, flip=0):
        x, y, z = ((h + k) % w for h, k, w in zip(here, d, WRAP))
        return ((x * 2 + y // 2) * 2 + (1 - core if flip else core), (y % 2) * 8 + z)

    near = [(STEP[u], 0) for u in STEP] + [((0, 0, 0), 1)]
    barrier = pltpu.get_barrier_semaphore()
    for d, f in near:
        pl.semaphore_signal(barrier, inc=1, device_id=device(d, f), device_id_type=MESH)

    row_best[...] = jnp.full(row_best.shape, -1.0, f32)
    col_best[...] = jnp.full(col_best.shape, -1.0, f32)
    for load in loads:
        load.wait()
    values = x_ref[...].astype(f32)
    scale = lax.rsqrt(jnp.sum(values * values, axis=1, keepdims=True) + 1e-06)
    buf[0, 0] = (values * scale).astype(bf16)
    line = lax.broadcasted_iota(jnp.int32, HEAD, 0)
    facts = jnp.zeros(HEAD, jnp.int32)
    for h in (0, 1):
        cl, rank = cl_ref[:, pl.ds(128 * h, 128)], ord_ref[:, pl.ds(128 * h, 128)]
        for n, row in ((0, cl), (2, rank // 256), (4, rank % 256)):
            facts = jnp.where(line == n + h, row, facts)
    head[0, 0] = facts.astype(f32).astype(bf16)

    pl.semaphore_wait(barrier, len(near))

    def hop(s, c):
        lo, n = CHUNKS[c]
        p, u = EDGE[s, c]
        return pltpu.make_async_remote_copy(
            src_ref=buf.at[0, p, pl.ds(lo, n)], dst_ref=buf.at[0, s, pl.ds(lo, n)],
            send_sem=link_out.at[s, c], recv_sem=link_in.at[s, c],
            device_id=device(minus(STEP[u])), device_id_type=MESH,
        )

    def head_hop(s):
        p, u = EDGE[s, 0]
        return pltpu.make_async_remote_copy(
            src_ref=head.at[0, p], dst_ref=head.at[0, s], send_sem=head_out.at[s], recv_sem=head_in.at[s],
            device_id=device(minus(STEP[u])), device_id_type=MESH,
        )

    def across(a, c):
        lo, n = CHUNKS[c]
        ways = [(buf.at[0, a, pl.ds(lo, n)], buf.at[1, a, pl.ds(lo, n)], pair_out.at[a, c], pair_in.at[a, c])]
        if c == 0:
            ways.append((head.at[0, a], head.at[1, a], pair_head_out.at[a], pair_head_in.at[a]))
        return [
            pltpu.make_async_remote_copy(
                src_ref=src, dst_ref=dst, send_sem=out, recv_sem=into,
                device_id=device((0, 0, 0), 1), device_id_type=MESH,
            )
            for src, dst, out, into in ways
        ]

    def send_on(s, c):
        for kid in sorted(KIDS.get((s, c), ()), key=lambda k: -height(k, c)):
            if c == 0:
                head_hop(kid).start()
            hop(kid, c).start()

    for c in range(NC):
        send_on(0, c)
    for c in range(NC):
        for copy in across(0, c):
            copy.start()

    lines = lax.broadcasted_iota(jnp.int32, (HEAD[0], 256), 0)
    lanes = lax.broadcasted_iota(jnp.int32, (HEAD[0], 256), 1)

    def spread(h):
        low = jnp.where(lines == h, 1.0, 0.0)
        high = jnp.where(lines == 2 + h, 256.0, jnp.where(lines == 4 + h, 1.0, 0.0))
        return jnp.where(lanes < 128, low, high).astype(bf16)

    def row_side(s):
        k = 0 if s == 0 else s - RING + 1
        for h in (0, 1):
            wide = lax.dot_general(head[0, s], spread(h), (((0,), (0,)), ((), ())), preferred_element_type=f32)
            row_cl[k, pl.ds(128 * h, 128), :] = wide[:, :128]
            row_ord[k, pl.ds(128 * h, 128), :] = wide[:, 128:]

    def col_side(a, half):
        top = head[half, a].astype(f32)
        for h in (0, 1):
            at = pl.ds(128 * h, 128)
            col_cl[a, half, :, at] = jnp.broadcast_to(top[h : h + 1], (8, 128))
            col_ord[a, half, :, at] = jnp.broadcast_to(top[2 + h : 3 + h] * 256.0 + top[4 + h : 5 + h], (8, 128))

    def slot(k):
        return slot_of(k) if isinstance(k, int) else jnp.where(k == 0, 0, k + RING - 1)

    def dot(item):
        *ks, a = item
        rows = jnp.concatenate([buf[0, slot(k)] for k in ks], axis=0)
        columns = jnp.concatenate([buf[0, a], buf[1, a]], axis=0)
        return lax.dot_general(rows, columns, (((1,), (1,)), ((), ())), preferred_element_type=f32)

    tiles = [(h, t) for h in (0, 1) for t in (0, 128)]

    def fold(ref, item, both=True):
        *ks, a = item
        cl = [col_cl[a, h, :, pl.ds(t, 128)] for h, t in tiles]
        rk = [col_ord[a, h, :, pl.ds(t, 128)] for h, t in tiles]
        top = [col_best[a, h, :, pl.ds(t, 128)] for h, t in tiles] if both else None
        for m, k in enumerate(ks):
            for i in range(ROWS // 8):
                at = pl.ds(8 * i, 8)
                mine, rank, best = row_cl[k, at, :], row_ord[k, at, :], row_best[k, at, :]
                for n in range(len(tiles)):
                    s = ref[pl.ds(ROWS * m + 8 * i, 8), pl.ds(128 * n, 128)]
                    same = jnp.where(mine == cl[n], s, -1.0)
                    later = rk[n] < rank
                    best = jnp.maximum(best, jnp.where(later, same, -1.0))
                    if both:
                        top[n] = jnp.maximum(top[n], jnp.where(later, -1.0, same))
                row_best[k, at, :] = best
        if both:
            for n, (h, t) in enumerate(tiles):
                col_best[a, h, :, pl.ds(t, 128)] = top[n]

    met = set()

    def meet(a):
        if a not in met:
            met.add(a)
            for c in range(NC):
                for copy in across(a, c):
                    copy.wait_recv()
            col_side(a, 1)

    def row_result(k):
        m = row_best[k]
        return jnp.concatenate(
            [jnp.max(m[128 * h : 128 * h + 128].T, axis=0, keepdims=True) for h in (0, 1)], axis=1
        )

    def col_result(a, h):
        return jnp.max(col_best[a, h], axis=0, keepdims=True)

    def home(n):
        s, f = HOME[n]
        return pltpu.make_async_remote_copy(
            src_ref=send_back.at[n], dst_ref=got_back.at[n], send_sem=home_out.at[n], recv_sem=home_in.at[n],
            device_id=device(SLOTS[s], f), device_id_type=MESH,
        )

    row_side(0)
    col_side(0, 0)
    meet(0)
    score_a[pl.ds(0, ROWS), :] = dot((0, 0))
    fold(score_a, (0, 0), both=False)

    parts = {s: 0 for s in range(NS)}
    for step in plan():
        if step[0] == "chunk":
            _, s, c = step
            hop(s, c).wait_recv()
            if c == 0:
                head_hop(s).wait_recv()
            send_on(s, c)
            if s < RING:
                for copy in across(s, c):
                    copy.start()
            parts[s] += 1
            if parts[s] == NC:
                if s < RING:
                    col_side(s, 0)
                elif s < RING + NR - 1:
                    row_side(s)
        elif step[0] == "home":
            n = step[1]
            s, f = HOME[n]
            send_back[n] = row_result(s - RING + 1) if s >= RING else col_result(s, f)
            home(n).start()
        elif step[0] == "first":
            meet(step[1][2])
            score_a[...] = dot(step[1])
        elif step[0] == "last":
            fold(score_a, step[1])
        else:
            table = step[1]
            for i in table[1:]:
                meet(i[2])
            n = len(table) - 1
            if n == 1:
                score_b[...] = dot(table[1])
                fold(score_a, table[0])
                score_a[...] = score_b[...]
                continue

            def pair(j, item):
                score_b[...] = dot(item(2 * j + 1))
                fold(score_a, item(2 * j))
                score_a[...] = dot(item(2 * j + 2))
                fold(score_b, item(2 * j + 1))

            if n == 2:
                pair(0, lambda i, table=table: table[i])
            else:
                def turn(j, carry, table=table, pair=pair):
                    pair(j, lambda i: tuple(pick([t[m] for t in table], i) for m in range(3)))
                    return carry

                lax.fori_loop(0, n // 2, turn, 0)

    best = jnp.maximum(row_result(0), col_result(0, 0))
    for s, c in EDGE:
        hop(s, c).wait_send()
        if c == 0:
            head_hop(s).wait_send()
    for a in range(RING):
        for c in range(NC):
            for copy in across(a, c):
                copy.wait_send()
    for n in range(len(HOME)):
        home(n).wait_recv()
        best = jnp.maximum(best, got_back[n])
    out_ref[...] = best
    for n in range(len(HOME)):
        home(n).wait_send()


def body(embeddings, cluster, order):
    f32, bf16, i32, nh = jnp.float32, jnp.bfloat16, jnp.int32, len(HOME)
    dma = pltpu.SemaphoreType.DMA
    out = pl.pallas_call(
        kernel,
        out_shape=jax.ShapeDtypeStruct((1, ROWS), f32),
        in_specs=[pl.BlockSpec(memory_space=pl.ANY)] * 3,
        out_specs=pl.BlockSpec(memory_space=pltpu.VMEM),
        scratch_shapes=[
            pltpu.VMEM((ROWS, WIDTH), bf16), pltpu.VMEM((1, ROWS), i32), pltpu.VMEM((1, ROWS), i32),
            pltpu.VMEM((2, NS, ROWS, WIDTH), bf16), pltpu.VMEM((2, NS, *HEAD), bf16),
            pltpu.VMEM((NR, ROWS, 128), f32), pltpu.VMEM((NR, ROWS, 128), f32),
            pltpu.VMEM((RING, 2, 8, ROWS), f32), pltpu.VMEM((RING, 2, 8, ROWS), f32),
            pltpu.VMEM((NR, ROWS, 128), f32), pltpu.VMEM((RING, 2, 8, ROWS), f32),
            pltpu.VMEM((2 * ROWS, 2 * ROWS), f32), pltpu.VMEM((2 * ROWS, 2 * ROWS), f32),
            pltpu.VMEM((nh, 1, ROWS), f32), pltpu.VMEM((nh, 1, ROWS), f32), dma((3,)),
            dma((NS, NC)), dma((NS, NC)), dma((NS,)), dma((NS,)), dma((RING, NC)), dma((RING, NC)), dma((RING,)), dma((RING,)),
            dma((nh,)), dma((nh,)),
        ],
        compiler_params=pltpu.CompilerParams(collective_id=0, has_side_effects=True, vmem_limit_bytes=60 * 2**20),
        cost_estimate=pl.CostEstimate(flops=10**10, bytes_accessed=2**20, transcendentals=0),
        name="nearest",
    )(embeddings, cluster.reshape(1, ROWS), order.reshape(1, ROWS))
    return out.reshape(ROWS)


def solution(mesh):
    return jax.shard_map(
        body,
        mesh=mesh,
        in_specs=(P(("grp", "blk"), None), P(("grp", "blk")), P(("grp", "blk"))),
        out_specs=P(("grp", "blk")),
        check_vma=False,
    )
```

```python
import jax
import jax.numpy as jnp
from jax import lax
from jax.experimental import pallas as pl
from jax.experimental.pallas import tpu as pltpu
from jax.sharding import PartitionSpec as P

MESH = pl.DeviceIdType.MESH
ROWS, WIDTH = 256, 512
HEAD = (16, 128)
CHUNKS = ((0, 128), (128, 128))
RING = 8
SLOTS = [(0, 0, z) for z in range(8)] + [
    (1, 0, 0), (0, 1, 0), (1, 1, 0), (1, 3, 0), (2, 0, 0), (0, 2, 0), (2, 1, 0), (3, 2, 0), (2, 2, 0),
]
NR = len(SLOTS) - RING + 1
SLOTS += [(3, 0, 0), (0, 3, 0)]
STEP = {"+x": (1, 0, 0), "-x": (3, 0, 0), "+y": (0, 1, 0), "-y": (0, 3, 0), "+z": (0, 0, 1), "-z": (0, 0, 7)}
FROM = {
    (0, 0, 1): ("+z", "+z"), (0, 0, 2): ("+z", "+z"), (0, 0, 3): ("+z", "+z"),
    (0, 0, 7): ("-z", "-z"), (0, 0, 6): ("-z", "-z"), (0, 0, 5): ("-z", "-z"), (0, 0, 4): ("+z", "-z"),
    (1, 0, 0): ("+x", "+x"), (3, 0, 0): ("-x", "-x"), (0, 1, 0): ("+y", "+y"), (0, 3, 0): ("-y", "-y"),
    (2, 0, 0): ("+x", "-x"), (0, 2, 0): ("+y", "-y"), (1, 1, 0): ("+x", "+y"), (1, 3, 0): ("-y", "-y"),
    (2, 1, 0): ("+x", "+y"), (3, 2, 0): ("-x", "-x"), (2, 2, 0): ("-x", "+y"),
}
NS = len(SLOTS)
NC = len(CHUNKS)
WRAP = (4, 4, 8)


def plus(a, b):
    return tuple((p + q) % w for p, q, w in zip(a, b, WRAP))


def minus(a):
    return tuple((-p) % w for p, w in zip(a, WRAP))


EDGE = {}
for s_ in range(1, NS):
    for c_ in range(NC):
        u_ = FROM[SLOTS[s_]][c_ % 2]
        EDGE[s_, c_] = (SLOTS.index(plus(SLOTS[s_], minus(STEP[u_]))), u_)
KIDS = {}
for (s_, c_), (p_, u_) in EDGE.items():
    KIDS.setdefault((p_, c_), []).append(s_)


def depth(s, c):
    return 0 if s == 0 else 1 + depth(EDGE[s, c][0], c)


def height(s, c):
    return max([0] + [1 + height(k, c) for k in KIDS.get((s, c), ())])


def arrivals(block=5.3, hop=2.0):
    at = {(0, c): 0.0 for c in range(NC)}
    free = {u: 0.0 for u in STEP}
    left = set(EDGE)
    while left:
        ready = [
            (max(at[EDGE[k][0], k[1]], free[EDGE[k][1]]), at[EDGE[k][0], k[1]], k[1], -height(*k), k[0])
            for k in left if (EDGE[k][0], k[1]) in at
        ]
        t, _, c, _, s = min(ready)
        free[EDGE[s, c][1]] = t + block / NC
        at[s, c] = t + block / NC + hop
        left.remove((s, c))
    return at


HALF_TURN = [s for s in range(RING, RING + NR - 1) if plus(SLOTS[s], SLOTS[s]) == (0, 0, 0)]
HOME = [(s, 0) for s in range(RING, RING + NR - 1)] + [(a, f) for a in range(1, RING) for f in (0, 1)] + [(0, 1)]
ITEM = 0.45
PAIR = 0.7


def slot_of(k):
    return 0 if k == 0 else k + RING - 1


def far(s):
    return sum(min(p, w - p) for p, w in zip(SLOTS[s], WRAP))


def reach(item):
    return max(far(slot_of(item[1])), far(slot_of(item[2])), far(item[3]))


def items(whole):
    out = []
    for a in range(RING):
        ks = [k for k in range(NR) if not (k == 0 and a in (0, 5, 6, 7)) and not (slot_of(k) in HALF_TURN and a > 4)]
        ks.sort(key=lambda k: (whole[slot_of(k)], k))
        if len(ks) % 2:
            ks.append(ks[-1])
        for i in range(0, len(ks), 2):
            at = max(whole[slot_of(ks[i])], whole[slot_of(ks[i + 1])], whole[a] + PAIR)
            out.append((at, ks[i], ks[i + 1], a))
    return sorted(out)


def plan():
    at = arrivals()
    seen = sorted((t, c, s) for (s, c), t in at.items() if s)
    whole = {s: max(at[s, c] for c in range(NC)) for s in range(NS)}
    todo = items(whole)
    steps, now, pending, home_left = [], 0.7, None, list(range(len(HOME)))

    def homes():
        left = [i[1:] for i in todo] + ([pending] if pending else [])
        done = []
        for n in list(home_left):
            s = HOME[n][0]
            if any(s == i[2] or s in (slot_of(i[0]), slot_of(i[1])) for i in left):
                continue
            done.append(n)
            home_left.remove(n)
        if done:
            steps.append(("home", done))

    while todo:
        while seen and seen[0][0] <= now:
            _, c, s = seen.pop(0)
            steps.append(("chunk", s, c))
        able = sorted((i for i in todo if i[0] <= now), key=lambda i: (i[0], -reach(i), i))
        if able:
            steps.append(("item", pending, able[0][1:]))
            now += ITEM if pending else ITEM / 2
            pending = able[0][1:]
            todo.remove(able[0])
            homes()
        elif pending is not None and (not seen or seen[0][0] > now + 0.5):
            steps.append(("item", pending, None))
            pending = None
            now += ITEM / 2
            homes()
        elif seen:
            now = max(now, seen[0][0])
        else:
            now += 0.1
    assert not seen
    if pending is not None:
        steps.append(("item", pending, None))
        pending = None
    homes()
    assert not home_left
    return steps


def kernel(x_hbm, cl_hbm, ord_hbm, out_ref, x_ref, cl_ref, ord_ref, buf, head, row_cl, row_ord, col_cl, col_ord, row_best,
           col_best, score_a, score_b, send_back, got_back, own_in, link_out, link_in, head_out, head_in, pair_out, pair_in,
           pair_head_out, pair_head_in, home_out, home_in):
    g, b = lax.axis_index("grp"), lax.axis_index("blk")
    core = g % 2
    here = (g // 4, ((g // 2) % 2) * 2 + b // 8, b % 8)
    f32, bf16 = jnp.float32, jnp.bfloat16

    loads = [
        pltpu.make_async_copy(a, v, own_in.at[n])
        for n, (a, v) in enumerate(((x_hbm, x_ref), (cl_hbm, cl_ref), (ord_hbm, ord_ref)))
    ]
    for load in loads:
        load.start()

    def device(d, flip=0):
        x, y, z = ((h + k) % w for h, k, w in zip(here, d, WRAP))
        return ((x * 2 + y // 2) * 2 + (1 - core if flip else core), (y % 2) * 8 + z)

    near = [(STEP[u], 0) for u in STEP] + [((0, 0, 0), 1)]
    barrier = pltpu.get_barrier_semaphore()
    for d, f in near:
        pl.semaphore_signal(barrier, inc=1, device_id=device(d, f), device_id_type=MESH)

    row_best[...] = jnp.full(row_best.shape, -1.0, f32)
    col_best[...] = jnp.full(col_best.shape, -1.0, f32)
    for load in loads:
        load.wait()
    values = x_ref[...].astype(f32)
    scale = lax.rsqrt(jnp.sum(values * values, axis=1, keepdims=True) + 1e-06)
    buf[0, 0] = (values * scale).astype(bf16)
    line = lax.broadcasted_iota(jnp.int32, HEAD, 0)
    facts = jnp.zeros(HEAD, jnp.int32)
    for h in (0, 1):
        cl, rank = cl_ref[:, pl.ds(128 * h, 128)], ord_ref[:, pl.ds(128 * h, 128)]
        for n, row in ((0, cl), (2, rank // 256), (4, rank % 256)):
            facts = jnp.where(line == n + h, row, facts)
    head[0, 0] = facts.astype(f32).astype(bf16)

    pl.semaphore_wait(barrier, len(near))

    def hop(s, c):
        lo, n = CHUNKS[c]
        p, u = EDGE[s, c]
        return pltpu.make_async_remote_copy(
            src_ref=buf.at[0, p, pl.ds(lo, n)], dst_ref=buf.at[0, s, pl.ds(lo, n)],
            send_sem=link_out.at[s, c], recv_sem=link_in.at[s, c],
            device_id=device(minus(STEP[u])), device_id_type=MESH,
        )

    def head_hop(s):
        p, u = EDGE[s, 0]
        return pltpu.make_async_remote_copy(
            src_ref=head.at[0, p], dst_ref=head.at[0, s], send_sem=head_out.at[s], recv_sem=head_in.at[s],
            device_id=device(minus(STEP[u])), device_id_type=MESH,
        )

    def across(a, c):
        lo, n = CHUNKS[c]
        ways = [(buf.at[0, a, pl.ds(lo, n)], buf.at[1, a, pl.ds(lo, n)], pair_out.at[a, c], pair_in.at[a, c])]
        if c == 0:
            ways.append((head.at[0, a], head.at[1, a], pair_head_out.at[a], pair_head_in.at[a]))
        return [
            pltpu.make_async_remote_copy(
                src_ref=src, dst_ref=dst, send_sem=out, recv_sem=into,
                device_id=device((0, 0, 0), 1), device_id_type=MESH,
            )
            for src, dst, out, into in ways
        ]

    def send_on(s, c):
        for kid in sorted(KIDS.get((s, c), ()), key=lambda k: -height(k, c)):
            if c == 0:
                head_hop(kid).start()
            hop(kid, c).start()

    for c in range(NC):
        send_on(0, c)
    for c in range(NC):
        for copy in across(0, c):
            copy.start()

    lines = lax.broadcasted_iota(jnp.int32, (HEAD[0], 256), 0)
    lanes = lax.broadcasted_iota(jnp.int32, (HEAD[0], 256), 1)

    def spread(h):
        low = jnp.where(lines == h, 1.0, 0.0)
        high = jnp.where(lines == 2 + h, 256.0, jnp.where(lines == 4 + h, 1.0, 0.0))
        return jnp.where(lanes < 128, low, high).astype(bf16)

    def row_side(s):
        k = 0 if s == 0 else s - RING + 1
        for h in (0, 1):
            wide = lax.dot_general(head[0, s], spread(h), (((0,), (0,)), ((), ())), preferred_element_type=f32)
            row_cl[k, pl.ds(128 * h, 128), :] = wide[:, :128]
            row_ord[k, pl.ds(128 * h, 128), :] = wide[:, 128:]

    def col_side(a, half):
        top = head[half, a].astype(f32)
        for h in (0, 1):
            at = pl.ds(128 * h, 128)
            col_cl[a, half, :, at] = jnp.broadcast_to(top[h : h + 1], (8, 128))
            col_ord[a, half, :, at] = jnp.broadcast_to(top[2 + h : 3 + h] * 256.0 + top[4 + h : 5 + h], (8, 128))

    def slot(k):
        return slot_of(k)

    def dot(item):
        *ks, a = item
        rows = jnp.concatenate([buf[0, slot(k)] for k in ks], axis=0)
        columns = jnp.concatenate([buf[0, a], buf[1, a]], axis=0)
        return lax.dot_general(rows, columns, (((1,), (1,)), ((), ())), preferred_element_type=f32)

    tiles = [(h, t) for h in (0, 1) for t in (0, 128)]

    def fold(ref, item, both=True):
        *ks, a = item
        cl = [col_cl[a, h, :, pl.ds(t, 128)] for h, t in tiles]
        rk = [col_ord[a, h, :, pl.ds(t, 128)] for h, t in tiles]
        top = [col_best[a, h, :, pl.ds(t, 128)] for h, t in tiles] if both else None
        for m, k in enumerate(ks):
            for i in range(ROWS // 8):
                at = pl.ds(8 * i, 8)
                mine, rank, best = row_cl[k, at, :], row_ord[k, at, :], row_best[k, at, :]
                for n in range(len(tiles)):
                    s = ref[pl.ds(ROWS * m + 8 * i, 8), pl.ds(128 * n, 128)]
                    same = jnp.where(mine == cl[n], s, -1.0)
                    later = rk[n] < rank
                    best = jnp.maximum(best, jnp.where(later, same, -1.0))
                    if both:
                        top[n] = jnp.maximum(top[n], jnp.where(later, -1.0, same))
                row_best[k, at, :] = best
        if both:
            for n, (h, t) in enumerate(tiles):
                col_best[a, h, :, pl.ds(t, 128)] = top[n]

    met = set()

    def meet(a):
        if a not in met:
            met.add(a)
            for c in range(NC):
                for copy in across(a, c):
                    copy.wait_recv()
            col_side(a, 1)

    def row_result(k):
        m = row_best[k]
        return jnp.concatenate(
            [jnp.max(m[128 * h : 128 * h + 128].T, axis=0, keepdims=True) for h in (0, 1)], axis=1
        )

    def col_result(a, h):
        return jnp.max(col_best[a, h], axis=0, keepdims=True)

    def home(n):
        s, f = HOME[n]
        return pltpu.make_async_remote_copy(
            src_ref=send_back.at[n], dst_ref=got_back.at[n], send_sem=home_out.at[n], recv_sem=home_in.at[n],
            device_id=device(SLOTS[s], f), device_id_type=MESH,
        )

    row_side(0)
    col_side(0, 0)
    meet(0)
    score_a[pl.ds(0, ROWS), :] = dot((0, 0))
    fold(score_a, (0, 0), both=False)

    parts = {s: 0 for s in range(NS)}
    scores, at = (score_a, score_b), 0
    for step in plan():
        if step[0] == "chunk":
            _, s, c = step
            hop(s, c).wait_recv()
            if c == 0:
                head_hop(s).wait_recv()
            send_on(s, c)
            if s < RING:
                for copy in across(s, c):
                    copy.start()
            parts[s] += 1
            if parts[s] == NC:
                if s < RING:
                    col_side(s, 0)
                elif s < RING + NR - 1:
                    row_side(s)
        elif step[0] == "home":
            for n in step[1]:
                s, f = HOME[n]
                send_back[n] = row_result(s - RING + 1) if s >= RING else col_result(s, f)
            for n in step[1]:
                home(n).start()
        else:
            _, old, new = step
            if new is not None:
                meet(new[2])
                scores[1 - at][...] = dot(new)
            if old is not None:
                fold(scores[at], old)
            at = 1 - at

    best = jnp.maximum(row_result(0), col_result(0, 0))
    for s, c in EDGE:
        hop(s, c).wait_send()
        if c == 0:
            head_hop(s).wait_send()
    for a in range(RING):
        for c in range(NC):
            for copy in across(a, c):
                copy.wait_send()
    for n in range(len(HOME)):
        home(n).wait_recv()
        best = jnp.maximum(best, got_back[n])
    out_ref[...] = best
    for n in range(len(HOME)):
        home(n).wait_send()


def body(embeddings, cluster, order):
    f32, bf16, i32, nh = jnp.float32, jnp.bfloat16, jnp.int32, len(HOME)
    dma = pltpu.SemaphoreType.DMA
    out = pl.pallas_call(
        kernel,
        out_shape=jax.ShapeDtypeStruct((1, ROWS), f32),
        in_specs=[pl.BlockSpec(memory_space=pl.ANY)] * 3,
        out_specs=pl.BlockSpec(memory_space=pltpu.VMEM),
        scratch_shapes=[
            pltpu.VMEM((ROWS, WIDTH), bf16), pltpu.VMEM((1, ROWS), i32), pltpu.VMEM((1, ROWS), i32),
            pltpu.VMEM((2, NS, ROWS, WIDTH), bf16), pltpu.VMEM((2, NS, *HEAD), bf16),
            pltpu.VMEM((NR, ROWS, 128), f32), pltpu.VMEM((NR, ROWS, 128), f32),
            pltpu.VMEM((RING, 2, 8, ROWS), f32), pltpu.VMEM((RING, 2, 8, ROWS), f32),
            pltpu.VMEM((NR, ROWS, 128), f32), pltpu.VMEM((RING, 2, 8, ROWS), f32),
            pltpu.VMEM((2 * ROWS, 2 * ROWS), f32), pltpu.VMEM((2 * ROWS, 2 * ROWS), f32),
            pltpu.VMEM((nh, 1, ROWS), f32), pltpu.VMEM((nh, 1, ROWS), f32), dma((3,)),
            dma((NS, NC)), dma((NS, NC)), dma((NS,)), dma((NS,)), dma((RING, NC)), dma((RING, NC)), dma((RING,)), dma((RING,)),
            dma((nh,)), dma((nh,)),
        ],
        compiler_params=pltpu.CompilerParams(collective_id=0, has_side_effects=True, vmem_limit_bytes=60 * 2**20),
        cost_estimate=pl.CostEstimate(flops=10**10, bytes_accessed=2**20, transcendentals=0),
        name="nearest",
    )(embeddings, cluster.reshape(1, ROWS), order.reshape(1, ROWS))
    return out.reshape(ROWS)


def solution(mesh):
    return jax.shard_map(
        body,
        mesh=mesh,
        in_specs=(P(("grp", "blk"), None), P(("grp", "blk")), P(("grp", "blk"))),
        out_specs=P(("grp", "blk")),
        check_vma=False,
    )
```

```python
import jax
import jax.numpy as jnp
from jax import lax
from jax.experimental import pallas as pl
from jax.experimental.pallas import tpu as pltpu
from jax.sharding import PartitionSpec as P

MESH = pl.DeviceIdType.MESH
ROWS, WIDTH = 256, 512
HEAD = (16, 128)
CHUNKS = ((0, 128), (128, 128))
RING = 8
SLOTS = [(0, 0, z) for z in range(8)] + [
    (1, 0, 0), (0, 1, 0), (3, 3, 0), (1, 3, 0), (2, 3, 0), (1, 2, 0), (2, 0, 0), (0, 2, 0), (2, 2, 0),
]
NR = len(SLOTS) - RING + 1
SLOTS += [(3, 0, 0), (0, 3, 0)]
STEP = {"+x": (1, 0, 0), "-x": (3, 0, 0), "+y": (0, 1, 0), "-y": (0, 3, 0), "+z": (0, 0, 1), "-z": (0, 0, 7)}
FROM = {
    (0, 0, 1): ("+z", "+z"), (0, 0, 2): ("+z", "+z"), (0, 0, 3): ("+z", "+z"),
    (0, 0, 7): ("-z", "-z"), (0, 0, 6): ("-z", "-z"), (0, 0, 5): ("-z", "-z"), (0, 0, 4): ("+z", "-z"),
    (1, 0, 0): ("+x", "+x"), (3, 0, 0): ("-x", "-x"), (0, 1, 0): ("+y", "+y"), (0, 3, 0): ("-y", "-y"),
    (3, 3, 0): ("-x", "-y"), (1, 3, 0): ("-y", "+x"), (2, 3, 0): ("-x", "+x"), (1, 2, 0): ("+x", "-y"),
    (2, 0, 0): ("-x", "+y"), (0, 2, 0): ("+y", "+y"), (2, 2, 0): ("-y", "+x"),
}
NS = len(SLOTS)
NC = len(CHUNKS)
WRAP = (4, 4, 8)


def plus(a, b):
    return tuple((p + q) % w for p, q, w in zip(a, b, WRAP))


def minus(a):
    return tuple((-p) % w for p, w in zip(a, WRAP))


EDGE = {}
for s_ in range(1, NS):
    for c_ in range(NC):
        u_ = FROM[SLOTS[s_]][c_ % 2]
        EDGE[s_, c_] = (SLOTS.index(plus(SLOTS[s_], minus(STEP[u_]))), u_)
KIDS = {}
for (s_, c_), (p_, u_) in EDGE.items():
    KIDS.setdefault((p_, c_), []).append(s_)


def depth(s, c):
    return 0 if s == 0 else 1 + depth(EDGE[s, c][0], c)


def height(s, c):
    return max([0] + [1 + height(k, c) for k in KIDS.get((s, c), ())])


def arrivals(block=5.3, hop=2.0):
    at = {(0, c): 0.0 for c in range(NC)}
    free = {u: 0.0 for u in STEP}
    left = set(EDGE)
    while left:
        ready = [
            (max(at[EDGE[k][0], k[1]], free[EDGE[k][1]]), at[EDGE[k][0], k[1]], k[1], -height(*k), k[0])
            for k in left if (EDGE[k][0], k[1]) in at
        ]
        t, _, c, _, s = min(ready)
        free[EDGE[s, c][1]] = t + block / NC
        at[s, c] = t + block / NC + hop
        left.remove((s, c))
    return at


HALF_TURN = [s for s in range(RING, RING + NR - 1) if plus(SLOTS[s], SLOTS[s]) == (0, 0, 0)]
HOME = [(s, 0) for s in range(RING, RING + NR - 1)] + [(a, f) for a in range(1, RING) for f in (0, 1)] + [(0, 1)]
ITEM = 0.45
PAIR = 0.7


def slot_of(k):
    return 0 if k == 0 else k + RING - 1


def far(s):
    return sum(min(p, w - p) for p, w in zip(SLOTS[s], WRAP))


def reach(item):
    return max(far(slot_of(item[1])), far(slot_of(item[2])), far(item[3]))


def items(whole):
    out = []
    for a in range(RING):
        ks = [k for k in range(NR) if not (k == 0 and a in (0, 5, 6, 7)) and not (slot_of(k) in HALF_TURN and a > 4)]
        ks.sort(key=lambda k: (whole[slot_of(k)], k))
        if len(ks) % 2:
            ks.append(ks[-1])
        for i in range(0, len(ks), 2):
            at = max(whole[slot_of(ks[i])], whole[slot_of(ks[i + 1])], whole[a] + PAIR)
            out.append((at, ks[i], ks[i + 1], a))
    return sorted(out)


def plan():
    at = arrivals()
    seen = sorted((t, c, s) for (s, c), t in at.items() if s)
    whole = {s: max(at[s, c] for c in range(NC)) for s in range(NS)}
    todo = items(whole)
    steps, now, pending, home_left = [], 0.7, None, list(range(len(HOME)))

    def homes():
        left = [i[1:] for i in todo] + ([pending] if pending else [])
        done = []
        for n in list(home_left):
            s = HOME[n][0]
            if any(s == i[2] or s in (slot_of(i[0]), slot_of(i[1])) for i in left):
                continue
            done.append(n)
            home_left.remove(n)
        if done:
            steps.append(("home", done))

    while todo:
        while seen and seen[0][0] <= now:
            _, c, s = seen.pop(0)
            steps.append(("chunk", s, c))
        able = sorted((i for i in todo if i[0] <= now), key=lambda i: (i[0], -reach(i), i))
        if able:
            steps.append(("item", pending, able[0][1:]))
            now += ITEM if pending else ITEM / 2
            pending = able[0][1:]
            todo.remove(able[0])
            homes()
        elif pending is not None and (not seen or seen[0][0] > now + 0.5):
            steps.append(("item", pending, None))
            pending = None
            now += ITEM / 2
            homes()
        elif seen:
            now = max(now, seen[0][0])
        else:
            now += 0.1
    assert not seen
    if pending is not None:
        steps.append(("item", pending, None))
        pending = None
    homes()
    assert not home_left
    return steps


def kernel(x_hbm, cl_hbm, ord_hbm, out_ref, x_ref, cl_ref, ord_ref, buf, head, row_cl, row_ord, col_cl, col_ord, row_best,
           col_best, score_a, score_b, send_back, got_back, own_in, link_out, link_in, head_out, head_in, pair_out, pair_in,
           pair_head_out, pair_head_in, home_out, home_in):
    g, b = lax.axis_index("grp"), lax.axis_index("blk")
    core = g % 2
    here = (g // 4, ((g // 2) % 2) * 2 + b // 8, b % 8)
    f32, bf16 = jnp.float32, jnp.bfloat16

    loads = [
        pltpu.make_async_copy(a, v, own_in.at[n])
        for n, (a, v) in enumerate(((x_hbm, x_ref), (cl_hbm, cl_ref), (ord_hbm, ord_ref)))
    ]
    for load in loads:
        load.start()

    def device(d, flip=0):
        x, y, z = ((h + k) % w for h, k, w in zip(here, d, WRAP))
        return ((x * 2 + y // 2) * 2 + (1 - core if flip else core), (y % 2) * 8 + z)

    near = [(STEP[u], 0) for u in STEP] + [((0, 0, 0), 1)]
    barrier = pltpu.get_barrier_semaphore()
    for d, f in near:
        pl.semaphore_signal(barrier, inc=1, device_id=device(d, f), device_id_type=MESH)

    row_best[...] = jnp.full(row_best.shape, -1.0, f32)
    col_best[...] = jnp.full(col_best.shape, -1.0, f32)
    for load in loads:
        load.wait()
    values = x_ref[...].astype(f32)
    scale = lax.rsqrt(jnp.sum(values * values, axis=1, keepdims=True) + 1e-06)
    buf[0, 0] = (values * scale).astype(bf16)
    line = lax.broadcasted_iota(jnp.int32, HEAD, 0)
    facts = jnp.zeros(HEAD, jnp.int32)
    for h in (0, 1):
        cl, rank = cl_ref[:, pl.ds(128 * h, 128)], ord_ref[:, pl.ds(128 * h, 128)]
        for n, row in ((0, cl), (2, rank // 256), (4, rank % 256)):
            facts = jnp.where(line == n + h, row, facts)
    head[0, 0] = facts.astype(f32).astype(bf16)

    pl.semaphore_wait(barrier, len(near))

    def hop(s, c):
        lo, n = CHUNKS[c]
        p, u = EDGE[s, c]
        return pltpu.make_async_remote_copy(
            src_ref=buf.at[0, p, pl.ds(lo, n)], dst_ref=buf.at[0, s, pl.ds(lo, n)],
            send_sem=link_out.at[s, c], recv_sem=link_in.at[s, c],
            device_id=device(minus(STEP[u])), device_id_type=MESH,
        )

    def head_hop(s):
        p, u = EDGE[s, 0]
        return pltpu.make_async_remote_copy(
            src_ref=head.at[0, p], dst_ref=head.at[0, s], send_sem=head_out.at[s], recv_sem=head_in.at[s],
            device_id=device(minus(STEP[u])), device_id_type=MESH,
        )

    def across(a, c):
        lo, n = CHUNKS[c]
        ways = [(buf.at[0, a, pl.ds(lo, n)], buf.at[1, a, pl.ds(lo, n)], pair_out.at[a, c], pair_in.at[a, c])]
        if c == 0:
            ways.append((head.at[0, a], head.at[1, a], pair_head_out.at[a], pair_head_in.at[a]))
        return [
            pltpu.make_async_remote_copy(
                src_ref=src, dst_ref=dst, send_sem=out, recv_sem=into,
                device_id=device((0, 0, 0), 1), device_id_type=MESH,
            )
            for src, dst, out, into in ways
        ]

    def send_on(s, c):
        for kid in sorted(KIDS.get((s, c), ()), key=lambda k: -height(k, c)):
            if c == 0:
                head_hop(kid).start()
            hop(kid, c).start()

    for c in range(NC):
        send_on(0, c)
    for c in range(NC):
        for copy in across(0, c):
            copy.start()

    lines = lax.broadcasted_iota(jnp.int32, (HEAD[0], 256), 0)
    lanes = lax.broadcasted_iota(jnp.int32, (HEAD[0], 256), 1)

    def spread(h):
        low = jnp.where(lines == h, 1.0, 0.0)
        high = jnp.where(lines == 2 + h, 256.0, jnp.where(lines == 4 + h, 1.0, 0.0))
        return jnp.where(lanes < 128, low, high).astype(bf16)

    def row_side(s):
        k = 0 if s == 0 else s - RING + 1
        for h in (0, 1):
            wide = lax.dot_general(head[0, s], spread(h), (((0,), (0,)), ((), ())), preferred_element_type=f32)
            row_cl[k, pl.ds(128 * h, 128), :] = wide[:, :128]
            row_ord[k, pl.ds(128 * h, 128), :] = wide[:, 128:]

    def col_side(a, half):
        top = head[half, a].astype(f32)
        for h in (0, 1):
            at = pl.ds(128 * h, 128)
            col_cl[a, half, :, at] = jnp.broadcast_to(top[h : h + 1], (8, 128))
            col_ord[a, half, :, at] = jnp.broadcast_to(top[2 + h : 3 + h] * 256.0 + top[4 + h : 5 + h], (8, 128))

    def slot(k):
        return slot_of(k)

    def dot(item):
        *ks, a = item
        rows = jnp.concatenate([buf[0, slot(k)] for k in ks], axis=0)
        columns = jnp.concatenate([buf[0, a], buf[1, a]], axis=0)
        return lax.dot_general(rows, columns, (((1,), (1,)), ((), ())), preferred_element_type=f32)

    tiles = [(h, t) for h in (0, 1) for t in (0, 128)]

    def fold(ref, item, both=True):
        *ks, a = item
        cl = [col_cl[a, h, :, pl.ds(t, 128)] for h, t in tiles]
        rk = [col_ord[a, h, :, pl.ds(t, 128)] for h, t in tiles]
        top = [col_best[a, h, :, pl.ds(t, 128)] for h, t in tiles] if both else None
        for m, k in enumerate(ks):
            for i in range(ROWS // 8):
                at = pl.ds(8 * i, 8)
                mine, rank, best = row_cl[k, at, :], row_ord[k, at, :], row_best[k, at, :]
                for n in range(len(tiles)):
                    s = ref[pl.ds(ROWS * m + 8 * i, 8), pl.ds(128 * n, 128)]
                    same = jnp.where(mine == cl[n], s, -1.0)
                    later = rk[n] < rank
                    best = jnp.maximum(best, jnp.where(later, same, -1.0))
                    if both:
                        top[n] = jnp.maximum(top[n], jnp.where(later, -1.0, same))
                row_best[k, at, :] = best
        if both:
            for n, (h, t) in enumerate(tiles):
                col_best[a, h, :, pl.ds(t, 128)] = top[n]

    met = set()

    def meet(a):
        if a not in met:
            met.add(a)
            for c in range(NC):
                for copy in across(a, c):
                    copy.wait_recv()
            col_side(a, 1)

    def row_result(k):
        m = row_best[k]
        return jnp.concatenate(
            [jnp.max(m[128 * h : 128 * h + 128].T, axis=0, keepdims=True) for h in (0, 1)], axis=1
        )

    def col_result(a, h):
        return jnp.max(col_best[a, h], axis=0, keepdims=True)

    def home(n):
        s, f = HOME[n]
        return pltpu.make_async_remote_copy(
            src_ref=send_back.at[n], dst_ref=got_back.at[n], send_sem=home_out.at[n], recv_sem=home_in.at[n],
            device_id=device(SLOTS[s], f), device_id_type=MESH,
        )

    row_side(0)
    col_side(0, 0)
    meet(0)
    score_a[pl.ds(0, ROWS), :] = dot((0, 0))
    fold(score_a, (0, 0), both=False)

    parts = {s: 0 for s in range(NS)}
    scores, at = (score_a, score_b), 0
    for step in plan():
        if step[0] == "chunk":
            _, s, c = step
            hop(s, c).wait_recv()
            if c == 0:
                head_hop(s).wait_recv()
            send_on(s, c)
            if s < RING:
                for copy in across(s, c):
                    copy.start()
            parts[s] += 1
            if parts[s] == NC:
                if s < RING:
                    col_side(s, 0)
                elif s < RING + NR - 1:
                    row_side(s)
        elif step[0] == "home":
            for n in step[1]:
                s, f = HOME[n]
                send_back[n] = row_result(s - RING + 1) if s >= RING else col_result(s, f)
            for n in step[1]:
                home(n).start()
        else:
            _, old, new = step
            if new is not None:
                meet(new[2])
                scores[1 - at][...] = dot(new)
            if old is not None:
                fold(scores[at], old)
            at = 1 - at

    best = jnp.maximum(row_result(0), col_result(0, 0))
    for s, c in EDGE:
        hop(s, c).wait_send()
        if c == 0:
            head_hop(s).wait_send()
    for a in range(RING):
        for c in range(NC):
            for copy in across(a, c):
                copy.wait_send()
    for n in range(len(HOME)):
        home(n).wait_recv()
        best = jnp.maximum(best, got_back[n])
    out_ref[...] = best
    for n in range(len(HOME)):
        home(n).wait_send()


def body(embeddings, cluster, order):
    f32, bf16, i32, nh = jnp.float32, jnp.bfloat16, jnp.int32, len(HOME)
    dma = pltpu.SemaphoreType.DMA
    out = pl.pallas_call(
        kernel,
        out_shape=jax.ShapeDtypeStruct((1, ROWS), f32),
        in_specs=[pl.BlockSpec(memory_space=pl.ANY)] * 3,
        out_specs=pl.BlockSpec(memory_space=pltpu.VMEM),
        scratch_shapes=[
            pltpu.VMEM((ROWS, WIDTH), bf16), pltpu.VMEM((1, ROWS), i32), pltpu.VMEM((1, ROWS), i32),
            pltpu.VMEM((2, NS, ROWS, WIDTH), bf16), pltpu.VMEM((2, NS, *HEAD), bf16),
            pltpu.VMEM((NR, ROWS, 128), f32), pltpu.VMEM((NR, ROWS, 128), f32),
            pltpu.VMEM((RING, 2, 8, ROWS), f32), pltpu.VMEM((RING, 2, 8, ROWS), f32),
            pltpu.VMEM((NR, ROWS, 128), f32), pltpu.VMEM((RING, 2, 8, ROWS), f32),
            pltpu.VMEM((2 * ROWS, 2 * ROWS), f32), pltpu.VMEM((2 * ROWS, 2 * ROWS), f32),
            pltpu.VMEM((nh, 1, ROWS), f32), pltpu.VMEM((nh, 1, ROWS), f32), dma((3,)),
            dma((NS, NC)), dma((NS, NC)), dma((NS,)), dma((NS,)), dma((RING, NC)), dma((RING, NC)), dma((RING,)), dma((RING,)),
            dma((nh,)), dma((nh,)),
        ],
        compiler_params=pltpu.CompilerParams(collective_id=0, has_side_effects=True, vmem_limit_bytes=60 * 2**20),
        cost_estimate=pl.CostEstimate(flops=10**10, bytes_accessed=2**20, transcendentals=0),
        name="nearest",
    )(embeddings, cluster.reshape(1, ROWS), order.reshape(1, ROWS))
    return out.reshape(ROWS)


def solution(mesh):
    return jax.shard_map(
        body,
        mesh=mesh,
        in_specs=(P(("grp", "blk"), None), P(("grp", "blk")), P(("grp", "blk"))),
        out_specs=P(("grp", "blk")),
        check_vma=False,
    )
```
